32 devices in a mesh: blk: 16 (over z, y, core), ax: 2 (over x).
Axes of the slice: x: 2, y: 2, z: 4, core: 2. Of those that a mesh axis runs over, the one named last changes fastest.
Arguments:
- pressure_guess: float32 [256, 48, 384], P('blk', 'ax'), may hold values from -6 to 6
- rhs: float32 [256, 48, 384], P('blk', 'ax'), may hold values from -16 to 16
- kappa: float32 [256, 48, 384], P('blk', 'ax'), may hold values from 1.5 to 4
- sigma: float32 [256, 48, 384], P('blk', 'ax'), may hold values from 0.05 to 0.4
Outputs:
- pressure: float32 [256, 48, 384], P('blk', 'ax')
The draws below stay inside these ranges and needn't reach their ends.
All inputs are finite; a program needn't handle non-finite values.
Results may differ from the reference program's by a relative error of at most 0.00002.
Values sent between devices are 32-bit elements; how exact they have to be, the bound alone decides.
A program may use at most 192 MiB of HBM per device.

```python
import math
from functools import reduce
import jax
import jax.numpy as jnp

NR = 384
NU = 2
NC = 4
NA = 256
NZ = 48


def draw_rhs(key, part):
    subkeys = jax.random.split(key, 4)
    sign_bit = jax.random.randint(subkeys[0], (), 0, 2)
    sign_value = (2 * sign_bit - 1).astype(jnp.float32)
    azimuth = jnp.arange(NA, dtype=jnp.float32)[:, None, None]
    axial = jnp.arange(NZ, dtype=jnp.float32)[None, :, None]
    radial = jnp.arange(NR, dtype=jnp.float32)[None, None, :]
    phases = jax.random.uniform(subkeys[1], (4,), jnp.float32, 0.0, 2.0 * math.pi)
    offset = 3.0
    amplitudes = jax.random.uniform(subkeys[2], (3,), jnp.float32, 1.0, 2.5)
    rough_part = 1.5 * jax.random.normal(subkeys[3], (NA, NZ, NR), jnp.float32)
    loop_part = sign_value * offset
    loop_part = loop_part + amplitudes[0] * jnp.cos(2.0 * math.pi * azimuth / NA + phases[0])
    loop_part = loop_part + amplitudes[1] * jnp.cos(4.0 * math.pi * azimuth / NA + phases[1])
    loop_part = loop_part + amplitudes[2] * jnp.cos(6.0 * math.pi * azimuth / NA + phases[2])
    axial_shape = 0.7 + 0.3 * jnp.sin(math.pi * (axial + 0.5) / NZ)
    radial_shape = 0.7 + 0.3 * jnp.cos(2.0 * math.pi * radial / NR + phases[3])
    smooth_field = loop_part * axial_shape * radial_shape + rough_part
    return jnp.clip(smooth_field, -16.0, 16.0)


def block_scale(stream_key, dims, shards, low, high):
    loudness = 1.0
    for axis_at, blocks in shards:
        steps = jax.random.uniform(jax.random.fold_in(jax.random.fold_in(stream_key, 6), axis_at), (blocks,), jnp.float32, low / len(shards), high / len(shards))
        loudness = loudness * jnp.repeat(jnp.exp(steps), dims[axis_at] // blocks).reshape((-1,) + (1,) * (len(dims) - 1 - axis_at))
    return loudness


def gaussian(stream_key, shape, deviation, bound, cuts=(), kind=jnp.bfloat16):
    gain = block_scale(stream_key, shape, cuts, -0.22, 0.18) if cuts else 1.0
    result = jax.random.normal(stream_key, shape, jnp.float32) * deviation * gain
    return jnp.minimum(jnp.maximum(result, -bound), bound).astype(kind)


def setup_inputs(seed: int = 0) -> dict:
    keys = jax.random.split(jax.random.key(seed), 5)
    pressure_guess = gaussian(keys[0], (NA, NZ, NR), 1.0, 6.0, ((0, 16), (1, 2)), jnp.float32)
    rhs = draw_rhs(jax.random.fold_in(keys[4], 71), 0)
    kappa = jnp.clip(jnp.exp(math.log(4.0) - 0.98082925 * jax.random.uniform(keys[2], (NA, NZ, NR), jnp.float32) ** block_scale(keys[2], (NA, NZ, NR), ((0, 16), (1, 2)), -0.2, 0.2)), 1.5, 4.0)
    sigma = jnp.clip(jnp.exp(math.log(0.4) - 2.0794415 * jax.random.uniform(keys[3], (NA, NZ, NR), jnp.float32) ** block_scale(keys[3], (NA, NZ, NR), ((0, 16), (1, 2)), -0.2, 0.2)), 0.05, 0.4)
    return dict(pressure_guess=pressure_guess, rhs=rhs, kappa=kappa, sigma=sigma)


omega_factor = 0.8


def neighbours(field):
    padded = jnp.pad(field, ((0, 0), (1, 1), (1, 1)))
    rows = field.shape[1]
    cols = field.shape[2]
    return [jnp.roll(field, 1, 0), jnp.roll(field, -1, 0),
            padded[:, 0:rows, 1:cols + 1], padded[:, 2:rows + 2, 1:cols + 1],
            padded[:, 1:rows + 1, 0:cols], padded[:, 1:rows + 1, 2:cols + 2]]


def tables(kappa, sigma):
    faces = [0.5 * (kappa + other) for other in neighbours(kappa)]
    diag = reduce(lambda left, right: left + right, faces) + sigma
    return faces, diag


def residual_of(field, target, faces, diag):
    near = neighbours(field)
    off = reduce(lambda left, right: left + right, [face * other for face, other in zip(faces, near)])
    return target - (diag * field - off)


def smooth(field, target, faces, diag, count):
    for sweep in range(count):
        field = field + omega_factor * residual_of(field, target, faces, diag) / diag
    return field


def coarsen(field):
    a, z, r = field.shape
    return field.reshape(a // 2, 2, z // 2, 2, r // 2, 2).mean(axis=(1, 3, 5))


def refine(field):
    return jnp.repeat(jnp.repeat(jnp.repeat(field, 2, 0), 2, 1), 2, 2)


def reference(pressure_guess, rhs, kappa, sigma):
    faces0, diag0 = tables(kappa, sigma)
    field = smooth(pressure_guess, rhs, faces0, diag0, NU)
    target1 = 4.0 * coarsen(residual_of(field, rhs, faces0, diag0))
    kappa1 = coarsen(kappa)
    sigma1 = 4.0 * coarsen(sigma)
    faces1, diag1 = tables(kappa1, sigma1)
    error1 = smooth(jnp.zeros_like(target1), target1, faces1, diag1, NU)
    target2 = 4.0 * coarsen(residual_of(error1, target1, faces1, diag1))
    kappa2 = coarsen(kappa1)
    sigma2 = 4.0 * coarsen(sigma1)
    faces2, diag2 = tables(kappa2, sigma2)
    error2 = smooth(jnp.zeros_like(target2), target2, faces2, diag2, NC)
    error1 = smooth(error1 + refine(error2), target1, faces1, diag1, NU)
    field = smooth(field + refine(error1), rhs, faces0, diag0, NU)
    return field
```

```python
import functools

import jax
import jax.numpy as jnp
import numpy as np
from jax import lax
from jax.experimental import pallas as pl
from jax.experimental.pallas import tpu as pltpu
from jax.sharding import PartitionSpec as P

OMEGA = 0.8
F32 = jnp.float32
BF16 = jnp.bfloat16


def up8(count):
    return -(-count // 8) * 8


def pad128(count):
    return -(-count // 128) * 128


class Level:
    def __init__(self, layers, rows, cols, halo):
        self.layers, self.rows, self.cols, self.halo = layers, rows, cols, halo
        self.lanes = pad128(cols)
        self.send_rows = up8(rows)
        self.ring = up8(rows + 2 * halo)
        self.deep = layers + 2 * halo

    def shape(self):
        return (self.deep, self.ring, self.lanes)


class Exchange:
    def __init__(self, level, widths, staged):
        self.level, self.widths, self.staged = level, widths, staged
        wide = max(widths.values())
        steps = range(1, -(-wide // level.layers) + 1)
        self.das = [s * d for d in steps for s in (1, -1)]
        self.blocks = []
        for da in self.das:
            for name, w in widths.items():
                c = min(w - (abs(da) - 1) * level.layers, level.layers)
                if c > 0:
                    base = (abs(da) - 1) * level.layers
                    if da > 0:
                        self.blocks.append((da, name, c, level.layers - c, -base - c))
                    else:
                        self.blocks.append((da, name, c, 0, level.layers + base))
        self.packs = []
        for dz in (1, -1):
            for da in [0] + self.das:
                pairs = []
                for name, w in widths.items():
                    for layer in range(level.layers):
                        if da > 0:
                            far, there = level.layers * da - layer, layer - level.layers * da
                        elif da < 0:
                            far, there = layer + 1 - level.layers * (da + 1), layer - level.layers * da
                        else:
                            far, there = 0, layer
                        for i in range(w - far):
                            if i >= level.rows:
                                continue
                            if dz > 0:
                                here_row, there_row = level.rows - 1 - i, level.ring - 1 - i
                            else:
                                here_row, there_row = i, level.rows + i
                            pairs.append((name, layer, here_row, there + level.halo, there_row))
                if pairs:
                    self.packs.append((da, dz, pairs))

    def count(self):
        return len(self.blocks) + len(self.packs)


def plan(layers, rows, cols):
    lv = [
        Level(layers, rows, cols, 2),
        Level(layers // 2, rows // 2, cols // 2, 5),
        Level(layers // 4, rows // 4, cols // 4, 6),
    ]
    ex = {
        "r1": Exchange(lv[0], {"k0": 2, "ua": 1, "s0": 1, "f0": 1}, False),
        "r2": Exchange(lv[0], {"ub": 1}, False),
        "r3": Exchange(lv[0], {"uc": 2}, False),
        "t1": Exchange(lv[1], {"k1": 5, "s1": 4}, True),
        "t2": Exchange(lv[2], {"k2": 6, "s2": 5}, True),
        "f1": Exchange(lv[1], {"f1": 4}, True),
        "f2": Exchange(lv[2], {"f2": 5}, True),
    }
    scratch = {}
    for name in ("k0", "s0", "f0", "ua", "ub", "uc", "ud", "ue", "ca0", "cz0", "cr0", "d0", "w0"):
        scratch[name] = pltpu.VMEM(lv[0].shape(), F32)
    for i in (1, 2):
        for name in ("k", "s", "f", "ca", "cz", "cr", "d", "w", "ea", "eb", "ec", "ed"):
            scratch[name + str(i)] = pltpu.VMEM(lv[i].shape(), F32)
        for name in ("k", "s", "f"):
            scratch["x" + name + str(i)] = pltpu.VMEM((lv[i].layers, lv[i].send_rows, lv[i].lanes), F32)
    scratch["res0"] = pltpu.VMEM((lv[0].layers, lv[0].send_rows, lv[0].lanes), F32)
    scratch["res1"] = pltpu.VMEM((lv[1].layers, lv[1].send_rows, lv[1].lanes), F32)
    total = 0
    for key, e in ex.items():
        e.key, e.first = key, total
        total += e.count()
        if e.staged:
            for b, (da, name, c, src, dst) in enumerate(e.blocks):
                scratch[f"{key}_b{b}"] = pltpu.VMEM((c, e.level.send_rows, e.level.lanes), F32)
        for p, (da, dz, pairs) in enumerate(e.packs):
            for side in "sr":
                scratch[f"{key}_{side}{p}"] = pltpu.VMEM((up8(len(pairs)), e.level.lanes), F32)
    scratch["ssem"] = pltpu.SemaphoreType.DMA((total,))
    scratch["rsem"] = pltpu.SemaphoreType.DMA((total,))
    scratch["lsem"] = pltpu.SemaphoreType.DMA((4,))
    return lv, ex, scratch


def halve_cols(fine, coarse):
    return (np.arange(fine.lanes)[:, None] // 2 == np.arange(coarse.lanes)[None, :]) & (
        np.arange(coarse.lanes)[None, :] < coarse.cols
    )


def halve_rows(fine, coarse):
    one = (np.arange(fine.send_rows)[None, :] // 2 == np.arange(coarse.send_rows)[:, None]) & (
        np.arange(fine.send_rows)[None, :] < fine.rows
    )
    return np.kron(np.eye(coarse.layers), one)


def double_rows(fine, coarse, count, width):
    one = np.zeros((fine.ring, coarse.ring))
    for z in range(-width, fine.rows + width):
        one[z % fine.ring, (z // 2) % coarse.ring] = 1.0
    return np.kron(np.eye(count), one)


def pieces(value):
    high = value.astype(BF16)
    rest = value - high.astype(F32)
    mid = rest.astype(BF16)
    low = (rest - mid.astype(F32)).astype(BF16)
    return high, mid, low


def right(value, matrix):
    return sum(jnp.dot(part, matrix, preferred_element_type=F32) for part in pieces(value))


def left(matrix, value):
    return sum(jnp.dot(matrix, part, preferred_element_type=F32) for part in pieces(value))


def kernel(lv, ex, names, nblk, nax, *refs):
    (g_in, f_in, k_in, s_in, c0, c1, h0, h1, b0, b1, d0, d1, out) = refs[:13]
    v = dict(zip(names, refs[13:]))
    blk, ax = lax.axis_index("blk"), lax.axis_index("ax")
    has = {1: ax < nax - 1, -1: ax > 0}

    def device(da, dz):
        return {"blk": lax.rem(blk + da + nblk, nblk), "ax": ax + dz}

    def when(dz, work):
        if dz == 0:
            work()
        else:
            pl.when(has[dz])(work)

    local = []
    for i, (src, name) in enumerate(((k_in, "k0"), (g_in, "ua"), (s_in, "s0"), (f_in, "f0"))):
        l0 = lv[0]
        local.append(
            pltpu.make_async_copy(
                src, v[name].at[pl.ds(l0.halo, l0.layers), pl.ds(0, l0.rows), :], v["lsem"].at[i]
            )
        )
        local[-1].start()

    l0 = lv[0]
    pad = (l0.deep, l0.ring - l0.rows, l0.lanes)
    for name in ("k0", "s0", "f0", "ua", "ub", "uc"):
        v[name][:, l0.rows : l0.ring, :] = jnp.zeros(pad, F32)
    for i in (1, 2):
        for name in ("k", "s", "f"):
            v[name + str(i)][...] = jnp.zeros(lv[i].shape(), F32)

    far = range(-2, 3)
    barrier = pltpu.get_barrier_semaphore()
    for dz in (0, 1, -1):
        def greet(dz=dz):
            for da in far:
                if (da, dz) != (0, 0):
                    pl.semaphore_signal(barrier, inc=1, device_id=device(da, dz))
        when(dz, greet)
    for copy in local:
        copy.wait()

    def messages(e):
        m = e.first
        for b, (da, name, c, src, dst) in enumerate(e.blocks):
            lev = e.level
            if e.staged:
                source, target = v["x" + name].at[pl.ds(src, c)], v[f"{e.key}_b{b}"]
            else:
                source = v[name].at[pl.ds(src + lev.halo, c), pl.ds(0, lev.rows), :]
                target = v[name].at[pl.ds(dst + lev.halo, c), pl.ds(0, lev.rows), :]
            yield da, 0, source, target, m, None, None
            m += 1
        for p, (da, dz, pairs) in enumerate(e.packs):
            yield da, dz, v[f"{e.key}_s{p}"], v[f"{e.key}_r{p}"], m, p, pairs
            m += 1

    def descriptor(message):
        da, dz, source, target, m, p, pairs = message
        return pltpu.make_async_remote_copy(
            source, target, v["ssem"].at[m], v["rsem"].at[m], device_id=device(da, dz)
        )

    def pack(e):
        for dz in (1, -1):
            def work(dz=dz):
                for da, dz_, source, target, m, p, pairs in messages(e):
                    if dz_ == dz:
                        for i, (name, layer, row, l_, r_) in enumerate(pairs):
                            if e.staged:
                                line = v["x" + name][layer, row : row + 1, :]
                            else:
                                line = v[name][layer + e.level.halo, row : row + 1, :]
                            source[i : i + 1, :] = line
            when(dz, work)

    def send(e):
        for dz in (1, -1, 0):
            def work(dz=dz):
                for message in messages(e):
                    if message[1] == dz:
                        descriptor(message).start()
            when(dz, work)

    def receive(e):
        for message in messages(e):
            if message[1] == 0:
                descriptor(message).wait_recv()
        if e.staged:
            lev = e.level
            for name in e.widths:
                v[name][lev.halo : lev.halo + lev.layers, 0 : lev.send_rows, :] = v["x" + name][...]
            for b, (da, name, c, src, dst) in enumerate(e.blocks):
                v[name][dst + lev.halo : dst + lev.halo + c, 0 : lev.send_rows, :] = v[f"{e.key}_b{b}"][...]
        for dz in (1, -1):
            def work(dz=dz):
                for message in messages(e):
                    if message[1] == dz:
                        descriptor(message).wait_recv()
                        for i, (name, l_, r_, layer, row) in enumerate(message[6]):
                            v[name][layer, row : row + 1, :] = message[3][i : i + 1, :]
            when(-dz, work)

    def sent(e):
        for dz in (0, 1, -1):
            def work(dz=dz):
                for message in messages(e):
                    if message[1] == dz:
                        descriptor(message).wait_send()
            when(dz, work)

    def loop(first, last, body):
        def step(i, carry):
            body(i)
            return carry
        lax.fori_loop(first, last, step, 0)

    def tables(i, width):
        lev = lv[i]
        k, s, ca, cz, cr, d, w = (v[n + str(i)] for n in ("k", "s", "ca", "cz", "cr", "d", "w"))
        lane = lax.broadcasted_iota(jnp.int32, (lev.ring, lev.lanes), 1)

        def body(l):
            mid, prev, after = k[l], k[l - 1], k[l + 1]
            up = pltpu.roll(mid, lev.ring - 1, 0)
            down = pltpu.roll(mid, 1, 0)
            inner = jnp.where(lane == lev.cols - 1, 0.0, pltpu.roll(mid, lev.lanes - 1, 1))
            outer = jnp.where(lane == 0, 0.0, pltpu.roll(mid, 1, 1))
            ca[l] = 0.5 * (mid + after)
            cz[l] = 0.5 * (mid + up)
            cr[l] = jnp.where(lane == lev.cols - 1, 0.0, 0.5 * (mid + inner))
            diag = 3.0 * mid + 0.5 * (((prev + after) + (up + down)) + (inner + outer)) + s[l]
            d[l] = diag
            w[l] = jnp.where(mid > 0.0, OMEGA / diag, 0.0)

        begin, end = lev.halo - width, lev.halo + lev.layers + width
        ca[begin - 1] = 0.5 * (k[begin - 1] + k[begin])
        loop(begin, end, body)

    def residual(i, u, l):
        lev = lv[i]
        f, ca, cz, cr, d = (v[n + str(i)] for n in ("f", "ca", "cz", "cr", "d"))
        mid = u[l]
        z, r = cz[l], cr[l]
        off = ca[l] * u[l + 1] + ca[l - 1] * u[l - 1]
        off += z * pltpu.roll(mid, lev.ring - 1, 0) + pltpu.roll(z * mid, 1, 0)
        off += r * pltpu.roll(mid, lev.lanes - 1, 1) + pltpu.roll(r * mid, 1, 1)
        return mid, f[l] - (d[l] * mid - off)

    def sweep(i, u, new, width):
        lev = lv[i]
        rows = lev.ring if width else lev.send_rows

        def body(l):
            mid, res = residual(i, u, l)
            value = mid + v["w" + str(i)][l] * res
            new[l, 0:rows, :] = value[0:rows]

        loop(lev.halo - width, lev.halo + lev.layers + width, body)

    def restrict(i, source, target, scale):
        fine, coarse = lv[i], lv[i + 1]
        value = source[...].reshape(coarse.layers, 2, fine.send_rows, fine.lanes)
        value = (value[:, 0] + value[:, 1]) * scale
        value = value.reshape(coarse.layers * fine.send_rows, fine.lanes)
        value = left((h0, h1)[i][...], right(value, (c0, c1)[i][...]))
        target[...] = value.reshape(coarse.layers, coarse.send_rows, coarse.lanes)

    def add_prolonged(i, base, error, new, width):
        fine, coarse = lv[i], lv[i + 1]
        edge = -(-width // 2)
        count = coarse.layers + 2 * edge
        value = error[coarse.halo - edge : coarse.halo + coarse.layers + edge]
        value = right(value.reshape(count * coarse.ring, coarse.lanes), (b0, b1)[i][...])
        value = left((d0, d1)[i][...], value).reshape(count, fine.ring, fine.lanes)
        for l in range(-width, fine.layers + width):
            new[l + fine.halo] = base[l + fine.halo] + value[l // 2 + edge]

    def residual_into(i, u, target):
        lev = lv[i]

        def body(l):
            target[l - lev.halo] = residual(i, u, l)[1][0 : lev.send_rows]

        loop(lev.halo, lev.halo + lev.layers, body)

    middle = v["k0"].at[pl.ds(l0.halo, l0.layers), pl.ds(0, l0.rows), :]
    middle_s = v["s0"].at[pl.ds(l0.halo, l0.layers), pl.ds(0, l0.rows), :]
    pack(ex["r1"])
    peers = len(far) - 1 + sum(jnp.where(has[dz], len(far), 0) for dz in (1, -1))
    pl.semaphore_wait(barrier, peers)
    send(ex["r1"])
    restrict(0, middle, v["xk1"], 0.125)
    restrict(0, middle_s, v["xs1"], 0.5)
    pack(ex["t1"])
    send(ex["t1"])
    restrict(1, v["xk1"], v["xk2"], 0.125)
    restrict(1, v["xs1"], v["xs2"], 0.5)
    pack(ex["t2"])
    send(ex["t2"])

    receive(ex["r1"])
    tables(0, 1)
    sweep(0, v["ua"], v["ub"], 0)
    pack(ex["r2"])
    send(ex["r2"])
    receive(ex["r2"])
    sweep(0, v["ub"], v["uc"], 0)
    pack(ex["r3"])
    send(ex["r3"])
    receive(ex["r3"])
    residual_into(0, v["uc"], v["res0"])
    restrict(0, v["res0"], v["xf1"], 0.5)
    pack(ex["f1"])
    send(ex["f1"])
    receive(ex["t1"])
    tables(1, 4)
    receive(ex["t2"])
    tables(2, 5)
    receive(ex["f1"])

    def first(i, width):
        lev = lv[i]

        def body(l):
            v["ea" + str(i)][l] = v["w" + str(i)][l] * v["f" + str(i)][l]

        loop(lev.halo - width, lev.halo + lev.layers + width, body)

    first(1, 4)
    sweep(1, v["ea1"], v["eb1"], 3)
    residual_into(1, v["eb1"], v["res1"])
    restrict(1, v["res1"], v["xf2"], 0.5)
    pack(ex["f2"])
    send(ex["f2"])
    receive(ex["f2"])
    first(2, 5)
    sweep(2, v["ea2"], v["eb2"], 4)
    sweep(2, v["eb2"], v["ec2"], 3)
    sweep(2, v["ec2"], v["ed2"], 2)
    add_prolonged(1, v["eb1"], v["ed2"], v["ec1"], 3)
    sweep(1, v["ec1"], v["ed1"], 2)
    sweep(1, v["ed1"], v["ea1"], 1)
    add_prolonged(0, v["uc"], v["ea1"], v["ud"], 2)
    sweep(0, v["ud"], v["ue"], 1)

    def last(l):
        mid, res = residual(0, v["ue"], l)
        out[l - l0.halo] = (mid + v["w0"][l] * res)[0 : l0.rows]

    loop(l0.halo, l0.halo + l0.layers, last)
    for e in ex.values():
        sent(e)


def solution(mesh):
    nblk, nax = mesh.shape["blk"], mesh.shape["ax"]

    def local(guess, rhs, kappa, sigma):
        layers, rows, cols = guess.shape
        lv, ex, scratch = plan(layers, rows, cols)
        mats = [
            halve_cols(lv[0], lv[1]),
            halve_cols(lv[1], lv[2]),
            halve_rows(lv[0], lv[1]),
            halve_rows(lv[1], lv[2]),
            halve_cols(lv[0], lv[1]).T,
            halve_cols(lv[1], lv[2]).T,
            double_rows(lv[0], lv[1], lv[1].layers + 2, 2),
            double_rows(lv[1], lv[2], lv[2].layers + 4, 3),
        ]
        mats = [jnp.asarray(m.astype(np.float32), BF16) for m in mats]
        anywhere = pl.BlockSpec(memory_space=pl.ANY)
        vmem = pl.BlockSpec(memory_space=pltpu.VMEM)
        return pl.pallas_call(
            functools.partial(kernel, lv, ex, list(scratch), nblk, nax),
            out_shape=jax.ShapeDtypeStruct(guess.shape, F32),
            in_specs=[anywhere] * 4 + [vmem] * len(mats),
            out_specs=vmem,
            scratch_shapes=list(scratch.values()),
            compiler_params=pltpu.CompilerParams(
                collective_id=0, has_side_effects=True, vmem_limit_bytes=48 * 2**20
            ),
        )(guess, rhs, kappa, sigma, *mats)

    spec = P("blk", "ax", None)
    return jax.shard_map(local, mesh=mesh, in_specs=(spec,) * 4, out_specs=spec, check_vma=False)
```

```python
import functools

import jax
import jax.numpy as jnp
import numpy as np
from jax import lax
from jax.experimental import pallas as pl
from jax.experimental.pallas import tpu as pltpu
from jax.sharding import PartitionSpec as P

OMEGA = 0.8
WIDE = 3
GROUPS = (4, 8, 14)
F32 = jnp.float32
BF16 = jnp.bfloat16


def up8(count):
    return -(-count // 8) * 8


def pad128(count):
    return -(-count // 128) * 128


class Level:
    def __init__(self, layers, rows, cols, halo):
        self.layers, self.rows, self.cols, self.halo = layers, rows, cols, halo
        self.lanes = pad128(cols)
        self.send_rows = up8(rows)
        self.ring = up8(rows + 2 * halo)
        self.deep = layers + 2 * halo

    def shape(self):
        return (self.deep, self.ring, self.lanes)


class Exchange:
    def __init__(self, level, widths, staged):
        self.level, self.widths, self.staged = level, widths, staged
        wide = max(widths.values())
        steps = range(1, -(-wide // level.layers) + 1)
        self.das = [s * d for d in steps for s in (1, -1)]
        self.blocks = []
        for da in self.das:
            for name, w in widths.items():
                c = min(w - (abs(da) - 1) * level.layers, level.layers)
                if c > 0:
                    base = (abs(da) - 1) * level.layers
                    if da > 0:
                        self.blocks.append((da, name, c, level.layers - c, -base - c))
                    else:
                        self.blocks.append((da, name, c, 0, level.layers + base))
        self.packs = []
        for dz in (1, -1):
            for da in [0] + self.das:
                pairs = []
                for name, w in widths.items():
                    for layer in range(level.layers):
                        if da > 0:
                            far, there = level.layers * da - layer, layer - level.layers * da
                        elif da < 0:
                            far, there = layer + 1 - level.layers * (da + 1), layer - level.layers * da
                        else:
                            far, there = 0, layer
                        for i in range(w - far):
                            if i >= level.rows:
                                continue
                            if dz > 0:
                                here_row, there_row = level.rows - 1 - i, level.ring - 1 - i
                            else:
                                here_row, there_row = i, level.rows + i
                            pairs.append((name, layer, here_row, there + level.halo, there_row))
                if pairs:
                    self.packs.append((da, dz, pairs))

    def count(self):
        return len(self.blocks) + len(self.packs)


def plan(layers, rows, cols):
    lv = [
        Level(layers, rows, cols, WIDE),
        Level(layers // 2, rows // 2, cols // 2, 5),
        Level(layers // 4, rows // 4, cols // 4, 6),
    ]
    ex = {
        "r1": Exchange(lv[0], {"k0": WIDE, "ua": WIDE, "s0": WIDE - 1, "f0": WIDE - 1}, False),
        "r3": Exchange(lv[0], {"ug": 2}, False),
        "t1": Exchange(lv[1], {"k1": 5, "s1": 4}, True),
        "t2": Exchange(lv[2], {"k2": 6, "s2": 5}, True),
        "f1": Exchange(lv[1], {"f1": 4}, True),
        "f2": Exchange(lv[2], {"f2": 5}, True),
    }
    scratch = {}
    for name in ("k0", "s0", "f0", "ua", "ub", "uc", "ug", "ud", "ue", "ca0", "cz0", "cr0", "d0", "w0"):
        scratch[name] = pltpu.VMEM(lv[0].shape(), F32)
    for i in (1, 2):
        for name in ("k", "s", "f", "ca", "cz", "cr", "d", "w", "ea", "eb", "ec", "ed"):
            scratch[name + str(i)] = pltpu.VMEM(lv[i].shape(), F32)
        for name in ("k", "s", "f"):
            scratch["x" + name + str(i)] = pltpu.VMEM((lv[i].layers, lv[i].send_rows, lv[i].lanes), F32)
    scratch["res0"] = pltpu.VMEM((lv[0].layers, lv[0].send_rows, lv[0].lanes), F32)
    scratch["res1"] = pltpu.VMEM((lv[1].layers, lv[1].send_rows, lv[1].lanes), F32)
    total = 0
    for key, e in ex.items():
        e.key, e.first = key, total
        total += e.count()
        if e.staged:
            for b, (da, name, c, src, dst) in enumerate(e.blocks):
                scratch[f"{key}_b{b}"] = pltpu.VMEM((c, e.level.send_rows, e.level.lanes), F32)
        for p, (da, dz, pairs) in enumerate(e.packs):
            for side in "sr":
                scratch[f"{key}_{side}{p}"] = pltpu.VMEM((up8(len(pairs)), e.level.lanes), F32)
    scratch["ssem"] = pltpu.SemaphoreType.DMA((total,))
    scratch["rsem"] = pltpu.SemaphoreType.DMA((total,))
    scratch["lsem"] = pltpu.SemaphoreType.DMA((5,))
    return lv, ex, scratch


def halve_cols(fine, coarse):
    return (np.arange(fine.lanes)[:, None] // 2 == np.arange(coarse.lanes)[None, :]) & (
        np.arange(coarse.lanes)[None, :] < coarse.cols
    )


def halve_rows(fine, coarse):
    one = (np.arange(fine.send_rows)[None, :] // 2 == np.arange(coarse.send_rows)[:, None]) & (
        np.arange(fine.send_rows)[None, :] < fine.rows
    )
    return np.kron(np.eye(coarse.layers), one)


def double_rows(fine, coarse, count, width):
    one = np.zeros((fine.ring, coarse.ring))
    for z in range(-width, fine.rows + width):
        one[z % fine.ring, (z // 2) % coarse.ring] = 1.0
    return np.kron(np.eye(count), one)


def pieces(value):
    high = value.astype(BF16)
    rest = value - high.astype(F32)
    mid = rest.astype(BF16)
    low = (rest - mid.astype(F32)).astype(BF16)
    return high, mid, low


def right(value, matrix):
    return sum(jnp.dot(part, matrix, preferred_element_type=F32) for part in pieces(value))


def left(matrix, value):
    return sum(jnp.dot(matrix, part, preferred_element_type=F32) for part in pieces(value))


def kernel(lv, ex, names, places, nblk, nax, *refs):
    g_in, f_in, k_in, s_in, m_in, out = refs[:6]
    v = dict(zip(names, refs[6:]))

    def matrix(i):
        first, rows, cols = places[i]
        return v["mats"][first : first + rows, 0:cols]

    blk, ax = lax.axis_index("blk"), lax.axis_index("ax")
    has = {1: ax < nax - 1, -1: ax > 0}

    def device(da, dz):
        return {"blk": lax.rem(blk + da + nblk, nblk), "ax": ax + dz}

    def when(dz, work):
        if dz == 0:
            work()
        else:
            pl.when(has[dz])(work)

    local = []
    for i, (src, name) in enumerate(((k_in, "k0"), (g_in, "ua"), (s_in, "s0"), (f_in, "f0"))):
        l0 = lv[0]
        local.append(
            pltpu.make_async_copy(
                src, v[name].at[pl.ds(l0.halo, l0.layers), pl.ds(0, l0.rows), :], v["lsem"].at[i]
            )
        )
        local[-1].start()

    mats_copy = pltpu.make_async_copy(m_in, v["mats"], v["lsem"].at[4])
    mats_copy.start()

    l0 = lv[0]
    pad = (l0.deep, l0.ring - l0.rows, l0.lanes)
    for name in ("k0", "s0", "f0", "ua", "ug"):
        v[name][:, l0.rows : l0.ring, :] = jnp.zeros(pad, F32)
    for i in (1, 2):
        for name in ("k", "s", "f"):
            v[name + str(i)][...] = jnp.zeros(lv[i].shape(), F32)

    far = range(-2, 3)
    barrier = pltpu.get_barrier_semaphore()
    for dz in (0, 1, -1):
        def greet(dz=dz):
            for da in far:
                if (da, dz) != (0, 0):
                    pl.semaphore_signal(barrier, inc=1, device_id=device(da, dz))
        when(dz, greet)
    for copy in local:
        copy.wait()

    def messages(e):
        m = e.first
        for b, (da, name, c, src, dst) in enumerate(e.blocks):
            lev = e.level
            if e.staged:
                source, target = v["x" + name].at[pl.ds(src, c)], v[f"{e.key}_b{b}"]
            else:
                source = v[name].at[pl.ds(src + lev.halo, c), pl.ds(0, lev.rows), :]
                target = v[name].at[pl.ds(dst + lev.halo, c), pl.ds(0, lev.rows), :]
            yield da, 0, source, target, m, None, None
            m += 1
        for p, (da, dz, pairs) in enumerate(e.packs):
            yield da, dz, v[f"{e.key}_s{p}"], v[f"{e.key}_r{p}"], m, p, pairs
            m += 1

    def descriptor(message):
        da, dz, source, target, m, p, pairs = message
        return pltpu.make_async_remote_copy(
            source, target, v["ssem"].at[m], v["rsem"].at[m], device_id=device(da, dz)
        )

    def pack(e):
        for dz in (1, -1):
            def work(dz=dz):
                for da, dz_, source, target, m, p, pairs in messages(e):
                    if dz_ == dz:
                        for i, (name, layer, row, l_, r_) in enumerate(pairs):
                            if e.staged:
                                line = v["x" + name][layer, row : row + 1, :]
                            else:
                                line = v[name][layer + e.level.halo, row : row + 1, :]
                            source[i : i + 1, :] = line
            when(dz, work)

    def send(e, packed=False):
        for message in messages(e):
            if message[1] == 0 and message[6] is None:
                descriptor(message).start()
        if not packed:
            pack(e)
        for dz in (1, -1):
            def work(dz=dz):
                for message in messages(e):
                    if message[1] == dz:
                        descriptor(message).start()
            when(dz, work)

    def receive(e):
        for message in messages(e):
            if message[1] == 0:
                descriptor(message).wait_recv()
        if e.staged:
            lev = e.level
            for name in e.widths:
                v[name][lev.halo : lev.halo + lev.layers, 0 : lev.send_rows, :] = v["x" + name][...]
            for b, (da, name, c, src, dst) in enumerate(e.blocks):
                v[name][dst + lev.halo : dst + lev.halo + c, 0 : lev.send_rows, :] = v[f"{e.key}_b{b}"][...]
        for dz in (1, -1):
            def work(dz=dz):
                for message in messages(e):
                    if message[1] == dz:
                        descriptor(message).wait_recv()
                        for i, (name, l_, r_, layer, row) in enumerate(message[6]):
                            v[name][layer, row : row + 1, :] = message[3][i : i + 1, :]
            when(-dz, work)

    def sent(e):
        for dz in (0, 1, -1):
            def work(dz=dz):
                for message in messages(e):
                    if message[1] == dz:
                        descriptor(message).wait_send()
            when(dz, work)

    def loop(i, first, last, body):
        group = max(g for g in range(1, GROUPS[i] + 1) if (last - first) % g == 0)
        if group == last - first:
            for l in range(first, last):
                body(l)
            return

        def step(n, carry):
            for j in range(group):
                body(first + n * group + j)
            return carry

        lax.fori_loop(0, (last - first) // group, step, 0)

    def tables(i, width):
        lev = lv[i]
        k, s, ca, cz, cr, d, w = (v[n + str(i)] for n in ("k", "s", "ca", "cz", "cr", "d", "w"))
        lane = lax.broadcasted_iota(jnp.int32, (lev.ring, lev.lanes), 1)

        def body(l):
            mid, prev, after = k[l], k[l - 1], k[l + 1]
            up = pltpu.roll(mid, lev.ring - 1, 0)
            down = pltpu.roll(mid, 1, 0)
            inner = jnp.where(lane == lev.cols - 1, 0.0, pltpu.roll(mid, lev.lanes - 1, 1))
            outer = jnp.where(lane == 0, 0.0, pltpu.roll(mid, 1, 1))
            ca[l] = 0.5 * (mid + after)
            cz[l] = 0.5 * (mid + up)
            cr[l] = jnp.where(lane == lev.cols - 1, 0.0, 0.5 * (mid + inner))
            diag = 3.0 * mid + 0.5 * (((prev + after) + (up + down)) + (inner + outer)) + s[l]
            d[l] = diag
            w[l] = jnp.where(mid > 0.0, OMEGA / diag, 0.0)

        begin, end = lev.halo - width, lev.halo + lev.layers + width
        ca[begin - 1] = 0.5 * (k[begin - 1] + k[begin])
        loop(i, begin, end, body)

    def residual(i, u, l):
        lev = lv[i]
        f, ca, cz, cr, d = (v[n + str(i)] for n in ("f", "ca", "cz", "cr", "d"))
        mid = u[l]
        z, r = cz[l], cr[l]
        off = ca[l] * u[l + 1] + ca[l - 1] * u[l - 1]
        off += z * pltpu.roll(mid, lev.ring - 1, 0) + pltpu.roll(z * mid, 1, 0)
        off += r * pltpu.roll(mid, lev.lanes - 1, 1) + pltpu.roll(r * mid, 1, 1)
        return mid, f[l] - (d[l] * mid - off)

    def sweep(i, u, new, width):
        lev = lv[i]
        rows = lev.ring if width else lev.send_rows

        def body(l):
            mid, res = residual(i, u, l)
            value = mid + v["w" + str(i)][l] * res
            new[l, 0:rows, :] = value[0:rows]

        loop(i, lev.halo - width, lev.halo + lev.layers + width, body)

    def restrict(i, source, target, scale):
        fine, coarse = lv[i], lv[i + 1]
        value = source[...].reshape(coarse.layers, 2, fine.send_rows, fine.lanes)
        value = (value[:, 0] + value[:, 1]) * scale
        value = value.reshape(coarse.layers * fine.send_rows, fine.lanes)
        value = left(matrix(2 + i), right(value, matrix(i)))
        target[...] = value.reshape(coarse.layers, coarse.send_rows, coarse.lanes)

    def add_prolonged(i, base, error, new, width):
        fine, coarse = lv[i], lv[i + 1]
        edge = -(-width // 2)
        count = coarse.layers + 2 * edge
        value = error[coarse.halo - edge : coarse.halo + coarse.layers + edge]
        value = right(value.reshape(count * coarse.ring, coarse.lanes), matrix(4 + i))
        value = left(matrix(6 + i), value).reshape(count, fine.ring, fine.lanes)
        for l in range(-width, fine.layers + width):
            new[l + fine.halo] = base[l + fine.halo] + value[l // 2 + edge]

    def residual_into(i, u, target):
        lev = lv[i]

        def body(l):
            target[l - lev.halo] = residual(i, u, l)[1][0 : lev.send_rows]

        loop(i, lev.halo, lev.halo + lev.layers, body)

    middle = v["k0"].at[pl.ds(l0.halo, l0.layers), pl.ds(0, l0.rows), :]
    middle_s = v["s0"].at[pl.ds(l0.halo, l0.layers), pl.ds(0, l0.rows), :]
    pack(ex["r1"])
    peers = len(far) - 1 + sum(jnp.where(has[dz], len(far), 0) for dz in (1, -1))
    pl.semaphore_wait(barrier, peers)
    send(ex["r1"], packed=True)
    mats_copy.wait()
    restrict(0, middle, v["xk1"], 0.125)
    restrict(0, middle_s, v["xs1"], 0.5)
    pack(ex["t1"])
    restrict(1, v["xk1"], v["xk2"], 0.125)
    restrict(1, v["xs1"], v["xs2"], 0.5)
    pack(ex["t2"])

    receive(ex["r1"])
    send(ex["t1"], packed=True)
    send(ex["t2"], packed=True)
    tables(0, WIDE - 1)
    sweep(0, v["ua"], v["ub"], WIDE - 1)
    sweep(0, v["ub"], v["uc"], WIDE - 2)
    inside = pl.ds(l0.halo, l0.layers)
    v["ug"][inside, 0 : l0.rows, :] = v["uc"][inside, 0 : l0.rows, :]
    if WIDE == 2:
        send(ex["r3"])
        receive(ex["r3"])
        residual_into(0, v["ug"], v["res0"])
    else:
        residual_into(0, v["uc"], v["res0"])
    restrict(0, v["res0"], v["xf1"], 0.5)
    send(ex["f1"])
    if WIDE == 3:
        send(ex["r3"])
    receive(ex["t1"])
    tables(1, 4)
    receive(ex["t2"])
    tables(2, 5)
    receive(ex["f1"])

    def first(i, width):
        lev = lv[i]

        def body(l):
            v["ea" + str(i)][l] = v["w" + str(i)][l] * v["f" + str(i)][l]

        loop(i, lev.halo - width, lev.halo + lev.layers + width, body)

    first(1, 4)
    sweep(1, v["ea1"], v["eb1"], 3)
    residual_into(1, v["eb1"], v["res1"])
    restrict(1, v["res1"], v["xf2"], 0.5)
    send(ex["f2"])
    receive(ex["f2"])
    first(2, 5)
    sweep(2, v["ea2"], v["eb2"], 4)
    sweep(2, v["eb2"], v["ec2"], 3)
    sweep(2, v["ec2"], v["ed2"], 2)
    add_prolonged(1, v["eb1"], v["ed2"], v["ec1"], 3)
    sweep(1, v["ec1"], v["ed1"], 2)
    sweep(1, v["ed1"], v["ea1"], 1)
    if WIDE == 3:
        receive(ex["r3"])
    add_prolonged(0, v["ug"], v["ea1"], v["ud"], 2)
    sweep(0, v["ud"], v["ue"], 1)

    def last(l):
        mid, res = residual(0, v["ue"], l)
        out[l - l0.halo] = (mid + v["w0"][l] * res)[0 : l0.rows]

    loop(0, l0.halo, l0.halo + l0.layers, last)
    for e in ex.values():
        sent(e)


def solution(mesh):
    nblk, nax = mesh.shape["blk"], mesh.shape["ax"]

    def local(guess, rhs, kappa, sigma):
        lv, ex, scratch = plan(*guess.shape)
        mats = [
            halve_cols(lv[0], lv[1]),
            halve_cols(lv[1], lv[2]),
            halve_rows(lv[0], lv[1]),
            halve_rows(lv[1], lv[2]),
            halve_cols(lv[0], lv[1]).T,
            halve_cols(lv[1], lv[2]).T,
            double_rows(lv[0], lv[1], lv[1].layers + 2, 2),
            double_rows(lv[1], lv[2], lv[2].layers + 4, 3),
        ]
        places, first = [], 0
        for m in mats:
            places.append((first, m.shape[0], m.shape[1]))
            first += -(-m.shape[0] // 16) * 16
        table = np.zeros((first, pad128(max(m.shape[1] for m in mats))), np.float32)
        for m, (at, rows, cols) in zip(mats, places):
            table[at : at + rows, 0:cols] = m
        table = jnp.asarray(table, BF16)
        scratch["mats"] = pltpu.VMEM(table.shape, BF16)
        anywhere = pl.BlockSpec(memory_space=pl.ANY)
        vmem = pl.BlockSpec(memory_space=pltpu.VMEM)
        return pl.pallas_call(
            functools.partial(kernel, lv, ex, list(scratch), places, nblk, nax),
            out_shape=jax.ShapeDtypeStruct(guess.shape, F32),
            in_specs=[anywhere] * 5,
            out_specs=vmem,
            scratch_shapes=list(scratch.values()),
            compiler_params=pltpu.CompilerParams(
                collective_id=0, has_side_effects=True, vmem_limit_bytes=61000 * 2**10
            ),
        )(guess, rhs, kappa, sigma, table)

    spec = P("blk", "ax", None)
    return jax.shard_map(local, mesh=mesh, in_specs=(spec,) * 4, out_specs=spec, check_vma=False)
```
